32 devices in a mesh: grp: 2 (over y), ex: 8 (over z, x), ffn: 2 (over core).
Axes of the slice: x: 2, y: 2, z: 4, core: 2. Of those that a mesh axis runs over, the one named last changes fastest.
Arguments:
- tokens_in: bfloat16 [8192, 4096], P(('grp', 'ex'), 'ffn'), parts along dimension 0, may hold values from -6 to 6
- grad_out: bfloat16 [8192, 14336], P(('grp', 'ex'), 'ffn'), parts along dimension 0, may hold values from -6 to 6
- proj_in: bfloat16 [4096, 32], P('ffn'), may hold values from -0.09375 to 0.09375
- proj_out: bfloat16 [14336, 32], P('ffn'), may hold values from -0.046875 to 0.046875
- segment_ids: int32 [16, 512], P(('grp', 'ex')), parts along dimension 0, may hold values from 0 to 15, never falling along the last dimension, each value on 1 to 64 neighbouring positions
- query_grads: float32 [256, 1024], P(('grp', 'ex')), parts along dimension 0, may hold values from -3 to 3
Outputs:
- scores: float32 [256, 128], P(('grp', 'ex')), parts along dimension 0
The draws below stay inside these ranges and needn't reach their ends.
There are 2 independent parts, one for each index of `grp`. The reference program is written for one: setup_inputs(seed, part) draws one part's arguments, and reference() takes and returns one part's arrays. A program takes and returns all parts, laid end to end along the dimension named above; an argument that names none is the same for every part. Nothing has to cross between parts.
Inputs may be any that keep to these rules, and one draw needn't show every extreme that they name: `segment_ids`: in each row the numbers never fall; each of the 16 examples of a row has 1 to 64 tokens, one exactly that many.
All inputs are finite; a program needn't handle non-finite values.
Results may differ from the reference program's by a relative error of at most 0.0003.
Values sent between devices are 32-bit elements; how exact they have to be, the bound alone decides.
A program may use at most 128 MiB of HBM per device.

```python
import math
import jax
import jax.numpy as jnp
import numpy as np
from jax import lax

D = 4096
FF = 14336
RANK = 32
TOK_DEV = 512
EX_DEV = 16
DIM = 1024
SHARDS = 8
TOKENS = 4096
EXAMPLES = 128
QUERIES = 128


def level_of(own_key, dims, split, low, largest):
    loudness = 1.0
    for position, blocks in split:
        draws = jax.random.uniform(jax.random.fold_in(jax.random.fold_in(own_key, 6), position), (blocks,), jnp.float32, low / len(split), largest / len(split))
        loudness = loudness * jnp.repeat(jnp.exp(draws), dims[position] // blocks).reshape((-1,) + (1,) * (len(dims) - 1 - position))
    return loudness


def length_profile(count, total, limit, lean):
    portions = [(1 << 20) // math.isqrt(rank ** lean) + 1 for rank in range(2, count + 1)]
    surplus, given = total - limit - (count - 1), [1] * (count - 1)
    while surplus > 0:
        candidates = [i for i in range(count - 1) if given[i] < limit]
        pool, left = sum([portions[i] for i in candidates]), surplus
        for i in candidates:
            addition = min(limit - given[i], max(1, left * portions[i] // pool), surplus)
            given[i] = given[i] + addition
            surplus = surplus - addition
    return np.array([limit] + given)


def ragged(own_key, amount, total, bound, lean):
    if amount == 2:
        one = jax.random.randint(own_key, (), max(1, total - bound), min(bound, total - 1) + 1)
        return jnp.stack([one, total - one])
    tallies = jnp.asarray(length_profile(amount, total, bound, lean), jnp.int32)
    couples = (amount - 1) // 2
    donor, receiver = tallies[1:1 + 2 * couples:2], tallies[2:2 + 2 * couples:2]
    slack = jnp.minimum(donor - 1, bound - receiver)
    passed = jax.random.randint(jax.random.fold_in(own_key, 1), (couples,), 0, 1 << 20) % (slack + 1)
    tallies = tallies.at[1:1 + 2 * couples:2].set(donor - passed).at[2:2 + 2 * couples:2].set(receiver + passed)
    return tallies[jax.random.permutation(jax.random.fold_in(own_key, 2), amount)]


def gaussian(key, extent, scale, bound, shards=(), kind=jnp.bfloat16):
    level = level_of(key, extent, shards, -0.22, 0.18) if shards else 1.0
    entries = jax.random.normal(key, extent, jnp.float32) * scale * level
    return jnp.minimum(jnp.maximum(entries, -bound), bound).astype(kind)


def setup_inputs(seed: int = 0, part: int = 0) -> dict:
    key_of = jax.random.split(jax.random.key(seed), 7)
    own_keys = jax.random.split(jax.random.fold_in(key_of[6], part), 7)
    tokens_in = gaussian(own_keys[0], (TOKENS, D), 1.0, 6.0, ((0, 8), (1, 2)))
    grad_out = gaussian(own_keys[1], (TOKENS, FF), 1.0, 6.0, ((0, 8), (1, 2)))
    proj_in = gaussian(key_of[2], (D, RANK), D ** -0.5, 0.09375, ((0, 2),))
    proj_out = gaussian(key_of[3], (FF, RANK), FF ** -0.5, 0.046875, ((0, 2),))
    segment_ids = jax.vmap(lambda own: jnp.searchsorted(jnp.cumsum(ragged(own, EX_DEV, TOK_DEV, 2 * TOK_DEV // EX_DEV, 1)), jnp.arange(TOK_DEV), side="right"))(jax.random.split(own_keys[4], SHARDS)).reshape((SHARDS, TOK_DEV)).astype(jnp.int32)
    query_grads = gaussian(own_keys[5], (QUERIES, DIM), 0.2, 3.0, ((0, 8),), jnp.float32)
    return {"tokens_in": tokens_in, "grad_out": grad_out, "proj_in": proj_in, "proj_out": proj_out, "segment_ids": segment_ids, "query_grads": query_grads}


def shard_grads(args):
    inputs, grads, seg, proj_in, proj_out = args
    out_side = jnp.dot(grads.astype(jnp.float32), proj_out.astype(jnp.float32), preferred_element_type=jnp.float32)
    in_side = jnp.dot(inputs.astype(jnp.float32), proj_in.astype(jnp.float32), preferred_element_type=jnp.float32)
    outer = (out_side[:, :, None] * in_side[:, None, :]).reshape(inputs.shape[0], RANK * RANK)
    sums = jax.ops.segment_sum(outer, seg, num_segments=EX_DEV)
    counts = jax.ops.segment_sum(jnp.ones(seg.shape, jnp.float32), seg, num_segments=EX_DEV)
    return sums / counts[:, None]

def reference(tokens_in, grad_out, proj_in, proj_out, segment_ids, query_grads):
    inputs = tokens_in.reshape(SHARDS, TOK_DEV, D)
    grads = grad_out.reshape(SHARDS, TOK_DEV, FF)

    def one_shard(index):
        return shard_grads((inputs[index], grads[index], segment_ids[index], proj_in, proj_out))
    example_grads = lax.map(one_shard, jnp.arange(SHARDS)).reshape(EXAMPLES, DIM)
    fisher_raw = jnp.dot(example_grads.T, example_grads, precision=lax.Precision.HIGHEST) / EXAMPLES
    damping = 0.1 * jnp.trace(fisher_raw) / DIM
    fisher = fisher_raw + damping * jnp.eye(DIM, dtype=jnp.float32)
    chol = jnp.linalg.cholesky(fisher)
    halfway = lax.linalg.triangular_solve(chol, query_grads.T, left_side=True, lower=True)
    precond = lax.linalg.triangular_solve(chol, halfway, left_side=True, lower=True, transpose_a=True)
    return jnp.dot(example_grads, precond, precision=lax.Precision.HIGHEST) / jnp.sqrt(jnp.float32(DIM))
```

```python
import jax
import jax.numpy as jnp
from jax import lax
from jax.sharding import PartitionSpec as P

EX_DEV = 16
HIGH = lax.Precision.HIGHEST


def example_means(tokens_in, grad_out, proj_in, proj_out, segment_ids):
    rank = proj_in.shape[1]
    width = rank * rank
    rows = tokens_in.shape[0]
    out_part = jnp.dot(grad_out, proj_out, preferred_element_type=jnp.float32)
    in_part = jnp.dot(tokens_in, proj_in, preferred_element_type=jnp.float32)
    out_side, in_side = lax.psum((out_part, in_part), "ffn")
    outer = (out_side[:, :, None] * in_side[:, None, :]).reshape(rows, width)
    labels = jnp.arange(EX_DEV, dtype=jnp.int32)
    member = (segment_ids[0][:, None] == labels[None, :]).astype(jnp.float32)
    counts = jnp.sum(member, axis=0)
    sums = lax.dot_general(member, outer, (((0,), (0,)), ((), ())), precision=HIGH)
    return sums / counts[:, None]


def primal(tokens_in, grad_out, proj_in, proj_out, segment_ids, query_grads):
    example_grads = example_means(tokens_in, grad_out, proj_in, proj_out, segment_ids)
    width = example_grads.shape[1]
    total = EX_DEV * lax.axis_size("ex")
    local_term = lax.dot_general(
        example_grads, example_grads, (((0,), (0,)), ((), ())), precision=HIGH
    )
    fisher_raw = lax.psum(local_term, "ex") / total
    damping = 0.1 * jnp.trace(fisher_raw) / width
    fisher = fisher_raw + damping * jnp.eye(width, dtype=jnp.float32)
    chol = jnp.linalg.cholesky(fisher)
    scale = jnp.sqrt(jnp.float32(width))
    halfway = lax.linalg.triangular_solve(chol, query_grads.T, left_side=True, lower=True)
    precond = lax.linalg.triangular_solve(
        chol, halfway, left_side=True, lower=True, transpose_a=True
    )
    gathered = lax.all_gather(precond, "ex", axis=1, tiled=True)
    return jnp.dot(example_grads, gathered, precision=HIGH) / scale


def dual(tokens_in, grad_out, proj_in, proj_out, segment_ids, query_grads):
    example_grads = example_means(tokens_in, grad_out, proj_in, proj_out, segment_ids)
    width = example_grads.shape[1]
    total = EX_DEV * lax.axis_size("ex")
    queries = lax.all_gather(query_grads, "ex", axis=0, tiled=True)
    everyone = lax.all_gather(example_grads, "ex", axis=0, tiled=True)
    gram = lax.dot_general(everyone, everyone, (((1,), (1,)), ((), ())), precision=HIGH) / total
    damping = 0.1 * jnp.trace(gram) / width
    gram = gram + damping * jnp.eye(total, dtype=jnp.float32)
    cross = lax.dot_general(everyone, queries, (((1,), (1,)), ((), ())), precision=HIGH)
    chol = jnp.linalg.cholesky(gram)
    mine = lax.axis_index("ex") * EX_DEV + jnp.arange(EX_DEV)
    pick = (jnp.arange(total)[:, None] == mine[None, :]).astype(jnp.float32)
    halfway = lax.linalg.triangular_solve(chol, pick, left_side=True, lower=True)
    rows = lax.linalg.triangular_solve(
        chol, halfway, left_side=True, lower=True, transpose_a=True
    )
    scores = lax.dot_general(rows, cross, (((0,), (0,)), ((), ())), precision=HIGH)
    return scores / jnp.sqrt(jnp.float32(width))


def solution(mesh):
    in_specs = (
        P(("grp", "ex"), "ffn"),
        P(("grp", "ex"), "ffn"),
        P("ffn", None),
        P("ffn", None),
        P(("grp", "ex"), None),
        P(("grp", "ex"), None),
    )
    out_specs = P(("grp", "ex"), None)

    def per_device(*args):
        width = args[2].shape[1] ** 2
        fewer = EX_DEV * mesh.shape["ex"] < width
        return (dual if fewer else primal)(*args)

    return jax.shard_map(
        per_device, mesh=mesh, in_specs=in_specs, out_specs=out_specs, check_vma=False
    )
```

```python
import functools

import jax
import jax.numpy as jnp
from jax import lax
from jax.experimental import pallas as pl
from jax.experimental.pallas import tpu as pltpu
from jax.sharding import PartitionSpec as P

EX_DEV = 16
HIGH = lax.Precision.HIGHEST


def example_means(tokens_in, grad_out, proj_in, proj_out, segment_ids):
    rank = proj_in.shape[1]
    width = rank * rank
    rows = tokens_in.shape[0]
    out_part = jnp.dot(grad_out, proj_out, preferred_element_type=jnp.float32)
    in_part = jnp.dot(tokens_in, proj_in, preferred_element_type=jnp.float32)
    out_side, in_side = lax.psum((out_part, in_part), "ffn")
    outer = (out_side[:, :, None] * in_side[:, None, :]).reshape(rows, width)
    labels = jnp.arange(EX_DEV, dtype=jnp.int32)
    member = (segment_ids[0][:, None] == labels[None, :]).astype(jnp.float32)
    counts = jnp.sum(member, axis=0)
    sums = lax.dot_general(member, outer, (((0,), (0,)), ((), ())), precision=HIGH)
    return sums / counts[:, None]


def primal(tokens_in, grad_out, proj_in, proj_out, segment_ids, query_grads):
    example_grads = example_means(tokens_in, grad_out, proj_in, proj_out, segment_ids)
    width = example_grads.shape[1]
    total = EX_DEV * lax.axis_size("ex")
    local_term = lax.dot_general(
        example_grads, example_grads, (((0,), (0,)), ((), ())), precision=HIGH
    )
    fisher_raw = lax.psum(local_term, "ex") / total
    damping = 0.1 * jnp.trace(fisher_raw) / width
    fisher = fisher_raw + damping * jnp.eye(width, dtype=jnp.float32)
    chol = jnp.linalg.cholesky(fisher)
    scale = jnp.sqrt(jnp.float32(width))
    halfway = lax.linalg.triangular_solve(chol, query_grads.T, left_side=True, lower=True)
    precond = lax.linalg.triangular_solve(
        chol, halfway, left_side=True, lower=True, transpose_a=True
    )
    gathered = lax.all_gather(precond, "ex", axis=1, tiled=True)
    return jnp.dot(example_grads, gathered, precision=HIGH) / scale


STEPS = 10
CHUNK = 1024
NT = (((1,), (1,)), ((), ()))


def dot(a, b):
    return jnp.dot(a, b, precision=HIGH, preferred_element_type=jnp.float32)


def dot_nt(a, b):
    return lax.dot_general(a, b, NT, precision=HIGH, preferred_element_type=jnp.float32)


def kernel(
    n, tok, grad, pin, pout, seg, qry, out,
    tok_v, grad_v, pin_v, pout_v, seg_v, mine, theirs, e_all, q_all, part, part_in,
    load_sem, chunk_sem, side_send, side_recv, e_send, e_recv, q_send, q_recv, p_send, p_recv,
):
    me, core = lax.axis_index("ex"), lax.axis_index("ffn")
    rank = pin.shape[1]
    half = rank // 2
    width = rank * rank
    cols = width // 2
    total = n * EX_DEV
    rows = pl.ds(pl.multiple_of(me * EX_DEV, EX_DEV), EX_DEV)

    loads = [
        pltpu.make_async_copy(
            qry.at[:, pl.ds(pl.multiple_of(core * cols, cols), cols)], q_all.at[rows], load_sem.at[0]
        ),
        pltpu.make_async_copy(pin, pin_v, load_sem.at[1]),
        pltpu.make_async_copy(tok, tok_v, load_sem.at[2]),
        pltpu.make_async_copy(pout, pout_v, load_sem.at[3]),
        pltpu.make_async_copy(seg, seg_v, load_sem.at[4]),
    ]
    chunks = [
        pltpu.make_async_copy(
            grad.at[:, pl.ds(k * CHUNK, CHUNK)], grad_v.at[:, pl.ds(k * CHUNK, CHUNK)], chunk_sem.at[k]
        )
        for k in range(grad.shape[1] // CHUNK)
    ]
    for copy in loads + chunks:
        copy.start()

    barrier = pltpu.get_barrier_semaphore()
    peers = [lax.rem(me + k, n) for k in range(1, n)]
    for peer in peers:
        pl.semaphore_signal(barrier, inc=1, device_id={"ex": peer}, device_id_type=pl.DeviceIdType.MESH)
    pl.semaphore_signal(barrier, inc=1, device_id={"ffn": 1 - core}, device_id_type=pl.DeviceIdType.MESH)
    pl.semaphore_wait(barrier, n)

    def spread(ref, send, recv):
        copies = [
            pltpu.make_async_remote_copy(
                src_ref=ref.at[rows], dst_ref=ref.at[rows],
                send_sem=send.at[k], recv_sem=recv.at[k],
                device_id={"ex": peer}, device_id_type=pl.DeviceIdType.MESH,
            )
            for k, peer in enumerate(peers)
        ]
        for copy in copies:
            copy.start()
        return copies

    def across(src, dst, send, recv):
        copy = pltpu.make_async_remote_copy(
            src_ref=src, dst_ref=dst, send_sem=send, recv_sem=recv,
            device_id={"ffn": 1 - core}, device_id_type=pl.DeviceIdType.MESH,
        )
        copy.start()
        return copy

    loads[0].wait()
    q_copies = spread(q_all, q_send, q_recv)

    loads[1].wait()
    loads[2].wait()
    in_part = jnp.dot(tok_v[...], pin_v[...], preferred_element_type=jnp.float32)
    mine[rank:, :] = in_part.T
    in_copy = across(
        mine.at[pl.ds(rank, rank)], theirs.at[pl.ds(half, rank)], side_send.at[0], side_recv.at[0]
    )

    loads[3].wait()
    acc = jnp.zeros((grad.shape[0], rank), jnp.float32)
    for k, copy in enumerate(chunks):
        copy.wait()
        span = slice(k * CHUNK, (k + 1) * CHUNK)
        acc += jnp.dot(grad_v[:, span], pout_v[span, :], preferred_element_type=jnp.float32)
    mine[:rank, :] = acc.T
    keep = pl.ds(pl.multiple_of(core * half, half), half)
    give = pl.ds(pl.multiple_of((1 - core) * half, half), half)
    out_copy = across(mine.at[give], theirs.at[pl.ds(0, half)], side_send.at[1], side_recv.at[1])

    loads[4].wait()
    labels = lax.broadcasted_iota(jnp.int32, (EX_DEV, seg_v.shape[1]), 0)
    member = (jnp.broadcast_to(seg_v[...], labels.shape) == labels).astype(jnp.float32)
    counts = jnp.sum(member, axis=1, keepdims=True)

    in_copy.wait()
    in_side = mine[rank:, :] + theirs[half:, :]
    in_tile = jnp.concatenate([in_side] * (128 // rank), axis=0)
    out_copy.wait()
    out_side = mine[keep, :] + theirs[:half, :]
    masked = jnp.concatenate([member * out_side[i : i + 1, :] for i in range(half)], axis=0)
    sums = dot_nt(masked, in_tile)
    per = 128 // rank
    place = lax.broadcasted_iota(jnp.int32, (EX_DEV, 128), 1) // rank
    for g in range(cols // 128):
        block = sums[g * per * EX_DEV : (g * per + 1) * EX_DEV]
        for k in range(1, per):
            row = (g * per + k) * EX_DEV
            block = jnp.where(place == k, sums[row : row + EX_DEV], block)
        e_all[rows, g * 128 : (g + 1) * 128] = block / counts
    e_copies = spread(e_all, e_send, e_recv)
    for copy in q_copies:
        copy.wait()
    for copy in e_copies:
        copy.wait()

    everyone = e_all[...]
    part[:, :total] = dot_nt(everyone, everyone)
    part[:, total:] = dot_nt(everyone, q_all[...])
    p_copy = across(part, part_in, p_send, p_recv)
    p_copy.wait()

    whole = part[...] + part_in[...]
    gram = whole[:, :total] * (1.0 / total)
    cross = whole[:, total:]
    r = lax.broadcasted_iota(jnp.int32, (total, total), 0)
    c = lax.broadcasted_iota(jnp.int32, (total, total), 1)
    eye = (r == c).astype(jnp.float32)
    trace = jnp.sum(jnp.sum(gram * eye, axis=1, keepdims=True), axis=0, keepdims=True)
    damping = (0.1 / width) * trace
    gram = gram + damping * eye
    bound = jnp.max(jnp.sum(jnp.abs(gram), axis=0, keepdims=True), axis=1, keepdims=True)
    bound = jnp.minimum(bound, trace + damping) * 1.0001
    low = damping / bound
    y = gram / bound
    x = eye / bound
    for _ in range(STEPS):
        scale = 4.0 / ((1.0 + low) * (1.0 + low))
        factor = scale * ((1.0 + low) * eye - y)
        both = dot(jnp.concatenate([y, x], axis=0), factor)
        y, x = both[:total], both[total:]
        low = jnp.minimum(scale * low, 1.0)
    part_in[:, :total] = x
    own = part_in[rows, :total]
    r16 = lax.broadcasted_iota(jnp.int32, (EX_DEV, total), 0)
    c16 = lax.broadcasted_iota(jnp.int32, (EX_DEV, total), 1)
    left = (r16 + me * EX_DEV == c16).astype(jnp.float32) - dot(own, gram)
    own = own + dot(left, x)
    out[...] = dot(own, cross) * (1.0 / width ** 0.5)


def dual(n, tokens_in, grad_out, proj_in, proj_out, segment_ids, query_grads):
    tok, rank = tokens_in.shape[0], proj_in.shape[1]
    cols = rank * rank // 2
    total = n * EX_DEV
    dma = pltpu.SemaphoreType.DMA
    return pl.pallas_call(
        functools.partial(kernel, n),
        out_shape=jax.ShapeDtypeStruct((EX_DEV, total), jnp.float32),
        in_specs=[pl.BlockSpec(memory_space=pl.ANY)] * 6,
        out_specs=pl.BlockSpec(memory_space=pltpu.VMEM),
        scratch_shapes=[
            pltpu.VMEM(tokens_in.shape, jnp.bfloat16),
            pltpu.VMEM(grad_out.shape, jnp.bfloat16),
            pltpu.VMEM(proj_in.shape, jnp.bfloat16),
            pltpu.VMEM(proj_out.shape, jnp.bfloat16),
            pltpu.VMEM(segment_ids.shape, jnp.int32),
            pltpu.VMEM((2 * rank, tok), jnp.float32),
            pltpu.VMEM((rank + rank // 2, tok), jnp.float32),
            pltpu.VMEM((total, cols), jnp.float32),
            pltpu.VMEM((total, cols), jnp.float32),
            pltpu.VMEM((total, 2 * total), jnp.float32),
            pltpu.VMEM((total, 2 * total), jnp.float32),
            dma((5,)),
            dma((grad_out.shape[1] // CHUNK,)),
            dma((2,)),
            dma((2,)),
            dma((n - 1,)),
            dma((n - 1,)),
            dma((n - 1,)),
            dma((n - 1,)),
            dma,
            dma,
        ],
        compiler_params=pltpu.CompilerParams(
            collective_id=0, has_side_effects=True, vmem_limit_bytes=50 * 2**20
        ),
    )(tokens_in, grad_out, proj_in, proj_out, segment_ids, query_grads)


def solution(mesh):
    in_specs = (
        P(("grp", "ex"), "ffn"),
        P(("grp", "ex"), "ffn"),
        P("ffn", None),
        P("ffn", None),
        P(("grp", "ex"), None),
        P(("grp", "ex"), None),
    )
    out_specs = P(("grp", "ex"), None)

    def per_device(*args):
        width = args[2].shape[1] ** 2
        n = mesh.shape["ex"]
        if EX_DEV * n == 128 and EX_DEV * n < width and mesh.shape["ffn"] == 2:
            return dual(n, *args)
        return primal(*args)

    return jax.shard_map(
        per_device, mesh=mesh, in_specs=in_specs, out_specs=out_specs, check_vma=False
    )
```

```python
import functools

import jax
import jax.numpy as jnp
from jax import lax
from jax.experimental import pallas as pl
from jax.experimental.pallas import tpu as pltpu
from jax.sharding import PartitionSpec as P

EX_DEV = 16
HIGH = lax.Precision.HIGHEST


def example_means(tokens_in, grad_out, proj_in, proj_out, segment_ids):
    rank = proj_in.shape[1]
    width = rank * rank
    rows = tokens_in.shape[0]
    out_part = jnp.dot(grad_out, proj_out, preferred_element_type=jnp.float32)
    in_part = jnp.dot(tokens_in, proj_in, preferred_element_type=jnp.float32)
    out_side, in_side = lax.psum((out_part, in_part), "ffn")
    outer = (out_side[:, :, None] * in_side[:, None, :]).reshape(rows, width)
    labels = jnp.arange(EX_DEV, dtype=jnp.int32)
    member = (segment_ids[0][:, None] == labels[None, :]).astype(jnp.float32)
    counts = jnp.sum(member, axis=0)
    sums = lax.dot_general(member, outer, (((0,), (0,)), ((), ())), precision=HIGH)
    return sums / counts[:, None]


def primal(tokens_in, grad_out, proj_in, proj_out, segment_ids, query_grads):
    example_grads = example_means(tokens_in, grad_out, proj_in, proj_out, segment_ids)
    width = example_grads.shape[1]
    total = EX_DEV * lax.axis_size("ex")
    local_term = lax.dot_general(
        example_grads, example_grads, (((0,), (0,)), ((), ())), precision=HIGH
    )
    fisher_raw = lax.psum(local_term, "ex") / total
    damping = 0.1 * jnp.trace(fisher_raw) / width
    fisher = fisher_raw + damping * jnp.eye(width, dtype=jnp.float32)
    chol = jnp.linalg.cholesky(fisher)
    scale = jnp.sqrt(jnp.float32(width))
    halfway = lax.linalg.triangular_solve(chol, query_grads.T, left_side=True, lower=True)
    precond = lax.linalg.triangular_solve(
        chol, halfway, left_side=True, lower=True, transpose_a=True
    )
    gathered = lax.all_gather(precond, "ex", axis=1, tiled=True)
    return jnp.dot(example_grads, gathered, precision=HIGH) / scale


STEPS = 10
CHUNK = 1024
NT = (((1,), (1,)), ((), ()))


def dot(a, b):
    return jnp.dot(a, b, precision=HIGH, preferred_element_type=jnp.float32)


def dot_nt(a, b):
    return lax.dot_general(a, b, NT, precision=HIGH, preferred_element_type=jnp.float32)


def kernel(
    n, tok, grad, pin, pout, seg, qry, out,
    tok_v, grad_v, pin_v, pout_v, seg_v, mine, theirs, e_all, q_all, part, part_in,
    load_sem, chunk_sem, side_send, side_recv, e_send, e_recv, q_send, q_recv, p_send, p_recv,
):
    me, core = lax.axis_index("ex"), lax.axis_index("ffn")
    rank = pin.shape[0]
    half = rank // 2
    width = rank * rank
    cols = width // 2
    total = n * EX_DEV
    rows = pl.ds(pl.multiple_of(me * EX_DEV, EX_DEV), EX_DEV)

    loads = [
        pltpu.make_async_copy(
            qry.at[:, pl.ds(pl.multiple_of(core * cols, cols), cols)], q_all.at[rows], load_sem.at[0]
        ),
        pltpu.make_async_copy(pin, pin_v, load_sem.at[1]),
        pltpu.make_async_copy(tok, tok_v, load_sem.at[2]),
        pltpu.make_async_copy(pout, pout_v, load_sem.at[3]),
        pltpu.make_async_copy(seg, seg_v, load_sem.at[4]),
    ]
    chunks = [
        pltpu.make_async_copy(
            grad.at[:, pl.ds(k * CHUNK, CHUNK)], grad_v.at[:, pl.ds(k * CHUNK, CHUNK)], chunk_sem.at[k]
        )
        for k in range(grad.shape[1] // CHUNK)
    ]
    for copy in loads + chunks:
        copy.start()

    barrier = pltpu.get_barrier_semaphore()
    peers = [lax.rem(me + k, n) for k in range(1, n)]
    for peer in peers:
        pl.semaphore_signal(barrier, inc=1, device_id={"ex": peer}, device_id_type=pl.DeviceIdType.MESH)
    pl.semaphore_signal(barrier, inc=1, device_id={"ffn": 1 - core}, device_id_type=pl.DeviceIdType.MESH)
    pl.semaphore_wait(barrier, n)

    def spread(ref, send, recv):
        copies = [
            pltpu.make_async_remote_copy(
                src_ref=ref.at[rows], dst_ref=ref.at[rows],
                send_sem=send.at[k], recv_sem=recv.at[k],
                device_id={"ex": peer}, device_id_type=pl.DeviceIdType.MESH,
            )
            for k, peer in enumerate(peers)
        ]
        for copy in copies:
            copy.start()
        return copies

    def across(src, dst, send, recv):
        copy = pltpu.make_async_remote_copy(
            src_ref=src, dst_ref=dst, send_sem=send, recv_sem=recv,
            device_id={"ffn": 1 - core}, device_id_type=pl.DeviceIdType.MESH,
        )
        copy.start()
        return copy

    loads[0].wait()
    q_copies = spread(q_all, q_send, q_recv)

    loads[1].wait()
    loads[2].wait()
    in_part = lax.dot_general(pin_v[...], tok_v[...], NT, preferred_element_type=jnp.float32)
    mine[rank:, :] = in_part
    in_copy = across(
        mine.at[pl.ds(rank, rank)], theirs.at[pl.ds(half, rank)], side_send.at[0], side_recv.at[0]
    )

    loads[3].wait()
    acc = jnp.zeros((rank, grad.shape[0]), jnp.float32)
    for k, copy in enumerate(chunks):
        copy.wait()
        span = slice(k * CHUNK, (k + 1) * CHUNK)
        acc += lax.dot_general(
            pout_v[:, span], grad_v[:, span], NT, preferred_element_type=jnp.float32
        )
    mine[:rank, :] = acc
    keep = pl.ds(pl.multiple_of(core * half, half), half)
    give = pl.ds(pl.multiple_of((1 - core) * half, half), half)
    out_copy = across(mine.at[give], theirs.at[pl.ds(0, half)], side_send.at[1], side_recv.at[1])

    loads[4].wait()
    labels = lax.broadcasted_iota(jnp.int32, (EX_DEV, seg_v.shape[1]), 0)
    member = (jnp.broadcast_to(seg_v[...], labels.shape) == labels).astype(jnp.float32)
    counts = jnp.sum(member, axis=1, keepdims=True)

    in_copy.wait()
    in_side = mine[rank:, :] + theirs[half:, :]
    in_tile = jnp.concatenate([in_side] * (128 // rank), axis=0)
    out_copy.wait()
    out_side = mine[keep, :] + theirs[:half, :]
    masked = jnp.concatenate([member * out_side[i : i + 1, :] for i in range(half)], axis=0)
    sums = dot_nt(masked, in_tile)
    per = 128 // rank
    place = lax.broadcasted_iota(jnp.int32, (EX_DEV, 128), 1) // rank
    for g in range(cols // 128):
        block = sums[g * per * EX_DEV : (g * per + 1) * EX_DEV]
        for k in range(1, per):
            row = (g * per + k) * EX_DEV
            block = jnp.where(place == k, sums[row : row + EX_DEV], block)
        e_all[rows, g * 128 : (g + 1) * 128] = block / counts
    e_copies = spread(e_all, e_send, e_recv)
    for copy in e_copies:
        copy.wait()

    everyone = e_all[...]
    part[:, :total] = dot_nt(everyone, everyone)
    k_copy = across(part.at[:, :total], part_in.at[:, :total], p_send.at[0], p_recv.at[0])
    for copy in q_copies:
        copy.wait()
    part[:, total:] = dot_nt(everyone, q_all[...])
    g_copy = across(part.at[:, total:], part_in.at[:, total:], p_send.at[1], p_recv.at[1])
    k_copy.wait()

    gram = (part[:, :total] + part_in[:, :total]) * (1.0 / total)
    r = lax.broadcasted_iota(jnp.int32, (total, total), 0)
    c = lax.broadcasted_iota(jnp.int32, (total, total), 1)
    eye = (r == c).astype(jnp.float32)
    trace = jnp.sum(jnp.sum(gram * eye, axis=1, keepdims=True), axis=0, keepdims=True)
    damping = (0.1 / width) * trace
    gram = gram + damping * eye
    bound = jnp.max(jnp.sum(jnp.abs(gram), axis=0, keepdims=True), axis=1, keepdims=True)
    bound = jnp.minimum(bound, trace + damping) * 1.0001
    low = damping / bound
    y = gram / bound
    x = eye / bound
    for _ in range(STEPS):
        scale = 4.0 / ((1.0 + low) * (1.0 + low))
        factor = scale * ((1.0 + low) * eye - y)
        both = dot(jnp.concatenate([y, x], axis=0), factor)
        y, x = both[:total], both[total:]
        low = jnp.minimum(scale * low, 1.0)
    part_in[:, :total] = x
    own = part_in[rows, :total]
    r16 = lax.broadcasted_iota(jnp.int32, (EX_DEV, total), 0)
    c16 = lax.broadcasted_iota(jnp.int32, (EX_DEV, total), 1)
    left = (r16 + me * EX_DEV == c16).astype(jnp.float32) - dot(own, gram)
    own = own + dot(left, x)
    g_copy.wait()
    cross = part[:, total:] + part_in[:, total:]
    out[...] = dot(own, cross) * (1.0 / width ** 0.5)


def dual(n, tokens_in, grad_out, proj_in, proj_out, segment_ids, query_grads):
    tok, rank = tokens_in.shape[0], proj_in.shape[1]
    cols = rank * rank // 2
    total = n * EX_DEV
    dma = pltpu.SemaphoreType.DMA
    return pl.pallas_call(
        functools.partial(kernel, n),
        out_shape=jax.ShapeDtypeStruct((EX_DEV, total), jnp.float32),
        in_specs=[pl.BlockSpec(memory_space=pl.ANY)] * 6,
        out_specs=pl.BlockSpec(memory_space=pltpu.VMEM),
        scratch_shapes=[
            pltpu.VMEM(tokens_in.shape, jnp.bfloat16),
            pltpu.VMEM(grad_out.shape, jnp.bfloat16),
            pltpu.VMEM(proj_in.shape[::-1], jnp.bfloat16),
            pltpu.VMEM(proj_out.shape[::-1], jnp.bfloat16),
            pltpu.VMEM(segment_ids.shape, jnp.int32),
            pltpu.VMEM((2 * rank, tok), jnp.float32),
            pltpu.VMEM((rank + rank // 2, tok), jnp.float32),
            pltpu.VMEM((total, cols), jnp.float32),
            pltpu.VMEM((total, cols), jnp.float32),
            pltpu.VMEM((total, 2 * total), jnp.float32),
            pltpu.VMEM((total, 2 * total), jnp.float32),
            dma((5,)),
            dma((grad_out.shape[1] // CHUNK,)),
            dma((2,)),
            dma((2,)),
            dma((n - 1,)),
            dma((n - 1,)),
            dma((n - 1,)),
            dma((n - 1,)),
            dma((2,)),
            dma((2,)),
        ],
        compiler_params=pltpu.CompilerParams(
            collective_id=0, has_side_effects=True, vmem_limit_bytes=60 * 2**20
        ),
    )(tokens_in, grad_out, proj_in.T, proj_out.T, segment_ids, query_grads)


def solution(mesh):
    in_specs = (
        P(("grp", "ex"), "ffn"),
        P(("grp", "ex"), "ffn"),
        P("ffn", None),
        P("ffn", None),
        P(("grp", "ex"), None),
        P(("grp", "ex"), None),
    )
    out_specs = P(("grp", "ex"), None)

    def per_device(*args):
        width = args[2].shape[1] ** 2
        n = mesh.shape["ex"]
        if EX_DEV * n == 128 and EX_DEV * n < width and mesh.shape["ffn"] == 2:
            return dual(n, *args)
        return primal(*args)

    return jax.shard_map(
        per_device, mesh=mesh, in_specs=in_specs, out_specs=out_specs, check_vma=False
    )
```

```python
import functools

import jax
import jax.numpy as jnp
from jax import lax
from jax.experimental import pallas as pl
from jax.experimental.pallas import tpu as pltpu
from jax.sharding import PartitionSpec as P

EX_DEV = 16
HIGH = lax.Precision.HIGHEST


def example_means(tokens_in, grad_out, proj_in, proj_out, segment_ids):
    rank = proj_in.shape[1]
    width = rank * rank
    rows = tokens_in.shape[0]
    out_part = jnp.dot(grad_out, proj_out, preferred_element_type=jnp.float32)
    in_part = jnp.dot(tokens_in, proj_in, preferred_element_type=jnp.float32)
    out_side, in_side = lax.psum((out_part, in_part), "ffn")
    outer = (out_side[:, :, None] * in_side[:, None, :]).reshape(rows, width)
    labels = jnp.arange(EX_DEV, dtype=jnp.int32)
    member = (segment_ids[0][:, None] == labels[None, :]).astype(jnp.float32)
    counts = jnp.sum(member, axis=0)
    sums = lax.dot_general(member, outer, (((0,), (0,)), ((), ())), precision=HIGH)
    return sums / counts[:, None]


def primal(tokens_in, grad_out, proj_in, proj_out, segment_ids, query_grads):
    example_grads = example_means(tokens_in, grad_out, proj_in, proj_out, segment_ids)
    width = example_grads.shape[1]
    total = EX_DEV * lax.axis_size("ex")
    local_term = lax.dot_general(
        example_grads, example_grads, (((0,), (0,)), ((), ())), precision=HIGH
    )
    fisher_raw = lax.psum(local_term, "ex") / total
    damping = 0.1 * jnp.trace(fisher_raw) / width
    fisher = fisher_raw + damping * jnp.eye(width, dtype=jnp.float32)
    chol = jnp.linalg.cholesky(fisher)
    scale = jnp.sqrt(jnp.float32(width))
    halfway = lax.linalg.triangular_solve(chol, query_grads.T, left_side=True, lower=True)
    precond = lax.linalg.triangular_solve(
        chol, halfway, left_side=True, lower=True, transpose_a=True
    )
    gathered = lax.all_gather(precond, "ex", axis=1, tiled=True)
    return jnp.dot(example_grads, gathered, precision=HIGH) / scale


STEPS = 10
CHUNK = 1024
NT = (((1,), (1,)), ((), ()))


def dot(a, b):
    return jnp.dot(a, b, precision=HIGH, preferred_element_type=jnp.float32)


def dot_nt(a, b):
    return lax.dot_general(a, b, NT, precision=HIGH, preferred_element_type=jnp.float32)


def kernel(
    n, tok, grad, pin, pout, seg, qry, out,
    tok_v, grad_v, pin_v, pout_v, seg_v, mine, theirs, e_all, q_all, part, part_in,
    load_sem, chunk_sem, side_send, side_recv, e_send, e_recv, q_send, q_recv, p_send, p_recv,
):
    me, core = lax.axis_index("ex"), lax.axis_index("ffn")
    rank = pin.shape[0]
    half = rank // 2
    width = rank * rank
    cols = width // 2
    total = n * EX_DEV
    rows = pl.ds(pl.multiple_of(me * EX_DEV, EX_DEV), EX_DEV)

    loads = [
        pltpu.make_async_copy(
            qry.at[:, pl.ds(pl.multiple_of(core * cols, cols), cols)], q_all.at[rows], load_sem.at[0]
        ),
        pltpu.make_async_copy(pin, pin_v, load_sem.at[1]),
        pltpu.make_async_copy(tok, tok_v, load_sem.at[2]),
        pltpu.make_async_copy(pout, pout_v, load_sem.at[3]),
        pltpu.make_async_copy(seg, seg_v, load_sem.at[4]),
    ]
    chunks = [
        pltpu.make_async_copy(
            grad.at[:, pl.ds(k * CHUNK, CHUNK)], grad_v.at[:, pl.ds(k * CHUNK, CHUNK)], chunk_sem.at[k]
        )
        for k in range(grad.shape[1] // CHUNK)
    ]
    for copy in loads + chunks:
        copy.start()

    barrier = pltpu.get_barrier_semaphore()
    peers = [lax.rem(me + k, n) for k in range(1, n)]
    for peer in peers:
        pl.semaphore_signal(barrier, inc=1, device_id={"ex": peer}, device_id_type=pl.DeviceIdType.MESH)
    pl.semaphore_signal(barrier, inc=1, device_id={"ffn": 1 - core}, device_id_type=pl.DeviceIdType.MESH)
    pl.semaphore_wait(barrier, n)

    def spread(ref, send, recv):
        copies = [
            pltpu.make_async_remote_copy(
                src_ref=ref.at[rows], dst_ref=ref.at[rows],
                send_sem=send.at[k], recv_sem=recv.at[k],
                device_id={"ex": peer}, device_id_type=pl.DeviceIdType.MESH,
            )
            for k, peer in enumerate(peers)
        ]
        for copy in copies:
            copy.start()
        return copies

    def across(src, dst, send, recv):
        copy = pltpu.make_async_remote_copy(
            src_ref=src, dst_ref=dst, send_sem=send, recv_sem=recv,
            device_id={"ffn": 1 - core}, device_id_type=pl.DeviceIdType.MESH,
        )
        copy.start()
        return copy

    loads[0].wait()
    q_copies = spread(q_all, q_send, q_recv)

    loads[1].wait()
    loads[2].wait()
    in_part = lax.dot_general(pin_v[...], tok_v[...], NT, preferred_element_type=jnp.float32)
    mine[rank:, :] = in_part
    in_copy = across(
        mine.at[pl.ds(rank, rank)], theirs.at[pl.ds(half, rank)], side_send.at[0], side_recv.at[0]
    )

    loads[3].wait()
    acc = jnp.zeros((rank, grad.shape[0]), jnp.float32)
    for k, copy in enumerate(chunks):
        copy.wait()
        span = slice(k * CHUNK, (k + 1) * CHUNK)
        acc += lax.dot_general(
            pout_v[:, span], grad_v[:, span], NT, preferred_element_type=jnp.float32
        )
    mine[:rank, :] = acc
    keep = pl.ds(pl.multiple_of(core * half, half), half)
    give = pl.ds(pl.multiple_of((1 - core) * half, half), half)
    out_copy = across(mine.at[give], theirs.at[pl.ds(0, half)], side_send.at[1], side_recv.at[1])

    loads[4].wait()
    labels = lax.broadcasted_iota(jnp.int32, (EX_DEV, seg_v.shape[1]), 0)
    member = (jnp.broadcast_to(seg_v[...], labels.shape) == labels).astype(jnp.float32)
    counts = jnp.sum(member, axis=1, keepdims=True)

    in_copy.wait()
    in_side = mine[rank:, :] + theirs[half:, :]
    in_tile = jnp.concatenate([in_side] * (128 // rank), axis=0)
    out_copy.wait()
    out_side = mine[keep, :] + theirs[:half, :]
    masked = jnp.concatenate([member * out_side[i : i + 1, :] for i in range(half)], axis=0)
    sums = dot_nt(masked, in_tile)
    per = 128 // rank
    place = lax.broadcasted_iota(jnp.int32, (EX_DEV, 128), 1) // rank
    for g in range(cols // 128):
        block = sums[g * per * EX_DEV : (g * per + 1) * EX_DEV]
        for k in range(1, per):
            row = (g * per + k) * EX_DEV
            block = jnp.where(place == k, sums[row : row + EX_DEV], block)
        e_all[rows, g * 128 : (g + 1) * 128] = block / counts
    e_copies = spread(e_all, e_send, e_recv)
    for copy in e_copies:
        copy.wait()

    everyone = e_all[...]
    part[:, :total] = dot_nt(everyone, everyone)
    k_copy = across(part.at[:, :total], part_in.at[:, :total], p_send.at[0], p_recv.at[0])
    for copy in q_copies:
        copy.wait()
    part[:, total:] = dot_nt(everyone, q_all[...])
    g_copy = across(part.at[:, total:], part_in.at[:, total:], p_send.at[1], p_recv.at[1])
    k_copy.wait()

    gram = (part[:, :total] + part_in[:, :total]) * (1.0 / total)
    r = lax.broadcasted_iota(jnp.int32, (total, total), 0)
    c = lax.broadcasted_iota(jnp.int32, (total, total), 1)
    eye = (r == c).astype(jnp.float32)
    trace = jnp.sum(jnp.sum(gram * eye, axis=1, keepdims=True), axis=0, keepdims=True)
    damping = (0.1 / width) * trace
    gram = gram + damping * eye
    bound = jnp.max(jnp.sum(jnp.abs(gram), axis=0, keepdims=True), axis=1, keepdims=True)
    bound = jnp.minimum(bound, trace + damping) * 1.0001
    low = damping / bound
    y = gram / bound
    x = eye / bound
    for _ in range(STEPS):
        scale = 4.0 / ((1.0 + low) * (1.0 + low))
        factor = scale * ((1.0 + low) * eye - y)
        both = dot(jnp.concatenate([y, x], axis=0), factor)
        y, x = both[:total], both[total:]
        low = jnp.minimum(scale * low, 1.0)
    part_in[:, :total] = x
    own = part_in[rows, :total]
    r16 = lax.broadcasted_iota(jnp.int32, (EX_DEV, total), 0)
    c16 = lax.broadcasted_iota(jnp.int32, (EX_DEV, total), 1)
    left = (r16 + me * EX_DEV == c16).astype(jnp.float32) - dot(own, gram)
    own = own + dot(left, x)
    g_copy.wait()
    cross = part[:, total:] + part_in[:, total:]
    out[...] = dot(own, cross) * (1.0 / width ** 0.5)


def dual(n, tokens_in, grad_out, proj_in, proj_out, segment_ids, query_grads):
    tok, rank = tokens_in.shape[0], proj_in.shape[1]
    cols = rank * rank // 2
    total = n * EX_DEV
    dma = pltpu.SemaphoreType.DMA
    return pl.pallas_call(
        functools.partial(kernel, n),
        out_shape=pltpu.VMEM((EX_DEV, total), jnp.float32),
        in_specs=[pl.BlockSpec(memory_space=pl.ANY)] * 6,
        out_specs=pl.BlockSpec(memory_space=pltpu.VMEM),
        scratch_shapes=[
            pltpu.VMEM(tokens_in.shape, jnp.bfloat16),
            pltpu.VMEM(grad_out.shape, jnp.bfloat16),
            pltpu.VMEM(proj_in.shape[::-1], jnp.bfloat16),
            pltpu.VMEM(proj_out.shape[::-1], jnp.bfloat16),
            pltpu.VMEM(segment_ids.shape, jnp.int32),
            pltpu.VMEM((2 * rank, tok), jnp.float32),
            pltpu.VMEM((rank + rank // 2, tok), jnp.float32),
            pltpu.VMEM((total, cols), jnp.float32),
            pltpu.VMEM((total, cols), jnp.float32),
            pltpu.VMEM((total, 2 * total), jnp.float32),
            pltpu.VMEM((total, 2 * total), jnp.float32),
            dma((5,)),
            dma((grad_out.shape[1] // CHUNK,)),
            dma((2,)),
            dma((2,)),
            dma((n - 1,)),
            dma((n - 1,)),
            dma((n - 1,)),
            dma((n - 1,)),
            dma((2,)),
            dma((2,)),
        ],
        compiler_params=pltpu.CompilerParams(
            collective_id=0, has_side_effects=True, vmem_limit_bytes=60 * 2**20
        ),
    )(tokens_in, grad_out, proj_in.T, proj_out.T, segment_ids, query_grads)


def solution(mesh):
    in_specs = (
        P(("grp", "ex"), "ffn"),
        P(("grp", "ex"), "ffn"),
        P("ffn", None),
        P("ffn", None),
        P(("grp", "ex"), None),
        P(("grp", "ex"), None),
    )
    out_specs = P(("grp", "ex"), None)

    def per_device(*args):
        width = args[2].shape[1] ** 2
        n = mesh.shape["ex"]
        if EX_DEV * n == 128 and EX_DEV * n < width and mesh.shape["ffn"] == 2:
            return dual(n, *args)
        return primal(*args)

    return jax.shard_map(
        per_device, mesh=mesh, in_specs=in_specs, out_specs=out_specs, check_vma=False
    )
```

```python
import functools

import jax
import jax.numpy as jnp
from jax import lax
from jax.experimental import pallas as pl
from jax.experimental.pallas import tpu as pltpu
from jax.sharding import PartitionSpec as P

EX_DEV = 16
HIGH = lax.Precision.HIGHEST


def example_means(tokens_in, grad_out, proj_in, proj_out, segment_ids):
    rank = proj_in.shape[1]
    width = rank * rank
    rows = tokens_in.shape[0]
    out_part = jnp.dot(grad_out, proj_out, preferred_element_type=jnp.float32)
    in_part = jnp.dot(tokens_in, proj_in, preferred_element_type=jnp.float32)
    out_side, in_side = lax.psum((out_part, in_part), "ffn")
    outer = (out_side[:, :, None] * in_side[:, None, :]).reshape(rows, width)
    labels = jnp.arange(EX_DEV, dtype=jnp.int32)
    member = (segment_ids[0][:, None] == labels[None, :]).astype(jnp.float32)
    counts = jnp.sum(member, axis=0)
    sums = lax.dot_general(member, outer, (((0,), (0,)), ((), ())), precision=HIGH)
    return sums / counts[:, None]


def primal(tokens_in, grad_out, proj_in, proj_out, segment_ids, query_grads):
    example_grads = example_means(tokens_in, grad_out, proj_in, proj_out, segment_ids)
    width = example_grads.shape[1]
    total = EX_DEV * lax.axis_size("ex")
    local_term = lax.dot_general(
        example_grads, example_grads, (((0,), (0,)), ((), ())), precision=HIGH
    )
    fisher_raw = lax.psum(local_term, "ex") / total
    damping = 0.1 * jnp.trace(fisher_raw) / width
    fisher = fisher_raw + damping * jnp.eye(width, dtype=jnp.float32)
    chol = jnp.linalg.cholesky(fisher)
    scale = jnp.sqrt(jnp.float32(width))
    halfway = lax.linalg.triangular_solve(chol, query_grads.T, left_side=True, lower=True)
    precond = lax.linalg.triangular_solve(
        chol, halfway, left_side=True, lower=True, transpose_a=True
    )
    gathered = lax.all_gather(precond, "ex", axis=1, tiled=True)
    return jnp.dot(example_grads, gathered, precision=HIGH) / scale


STEPS = 9
CHUNK = 1792
NT = (((1,), (1,)), ((), ()))


def dot(a, b):
    return jnp.dot(a, b, precision=HIGH, preferred_element_type=jnp.float32)


def dot_nt(a, b):
    return lax.dot_general(a, b, NT, precision=HIGH, preferred_element_type=jnp.float32)


def kernel(
    n, tok, grad, pin, pout, seg, qry, out,
    tok_v, grad_v, pin_v, pout_v, seg_v, mine, theirs, e_all, q_all, part, part_in,
    load_sem, chunk_sem, side_send, side_recv, e_send, e_recv, q_send, q_recv, p_send, p_recv,
):
    me, core = lax.axis_index("ex"), lax.axis_index("ffn")
    rank = pin.shape[0]
    half = rank // 2
    width = rank * rank
    cols = width // 2
    total = n * EX_DEV
    rows = pl.ds(pl.multiple_of(me * EX_DEV, EX_DEV), EX_DEV)

    loads = [
        pltpu.make_async_copy(
            qry.at[:, pl.ds(pl.multiple_of(core * cols, cols), cols)], q_all.at[rows], load_sem.at[0]
        ),
        pltpu.make_async_copy(pin, pin_v, load_sem.at[1]),
        pltpu.make_async_copy(tok, tok_v, load_sem.at[2]),
        pltpu.make_async_copy(pout, pout_v, load_sem.at[3]),
        pltpu.make_async_copy(seg, seg_v, load_sem.at[4]),
    ]
    chunks = [
        pltpu.make_async_copy(
            grad.at[:, pl.ds(k * CHUNK, CHUNK)], grad_v.at[:, pl.ds(k * CHUNK, CHUNK)], chunk_sem.at[k]
        )
        for k in range(grad.shape[1] // CHUNK)
    ]
    for copy in loads + chunks:
        copy.start()

    barrier = pltpu.get_barrier_semaphore()
    peers = [lax.rem(me + k, n) for k in range(1, n)]
    for peer in peers:
        pl.semaphore_signal(barrier, inc=1, device_id={"ex": peer}, device_id_type=pl.DeviceIdType.MESH)
    pl.semaphore_signal(barrier, inc=1, device_id={"ffn": 1 - core}, device_id_type=pl.DeviceIdType.MESH)
    pl.semaphore_wait(barrier, n)

    def spread(ref, send, recv):
        copies = [
            pltpu.make_async_remote_copy(
                src_ref=ref.at[rows], dst_ref=ref.at[rows],
                send_sem=send.at[k], recv_sem=recv.at[k],
                device_id={"ex": peer}, device_id_type=pl.DeviceIdType.MESH,
            )
            for k, peer in enumerate(peers)
        ]
        for copy in copies:
            copy.start()
        return copies

    def across(src, dst, send, recv):
        copy = pltpu.make_async_remote_copy(
            src_ref=src, dst_ref=dst, send_sem=send, recv_sem=recv,
            device_id={"ffn": 1 - core}, device_id_type=pl.DeviceIdType.MESH,
        )
        copy.start()
        return copy

    loads[0].wait()
    q_copies = spread(q_all, q_send, q_recv)

    loads[1].wait()
    loads[2].wait()
    in_part = lax.dot_general(pin_v[...], tok_v[...], NT, preferred_element_type=jnp.float32)
    mine[rank:, :] = in_part
    in_copy = across(
        mine.at[pl.ds(rank, rank)], theirs.at[pl.ds(half, rank)], side_send.at[0], side_recv.at[0]
    )

    loads[3].wait()
    acc = jnp.zeros((rank, grad.shape[0]), jnp.float32)
    for k, copy in enumerate(chunks):
        copy.wait()
        span = slice(k * CHUNK, (k + 1) * CHUNK)
        acc += lax.dot_general(
            pout_v[:, span], grad_v[:, span], NT, preferred_element_type=jnp.float32
        )
    mine[:rank, :] = acc
    keep = pl.ds(pl.multiple_of(core * half, half), half)
    give = pl.ds(pl.multiple_of((1 - core) * half, half), half)
    out_copy = across(mine.at[give], theirs.at[pl.ds(0, half)], side_send.at[1], side_recv.at[1])

    loads[4].wait()
    labels = lax.broadcasted_iota(jnp.int32, (EX_DEV, seg_v.shape[1]), 0)
    member = (jnp.broadcast_to(seg_v[...], labels.shape) == labels).astype(jnp.float32)
    counts = jnp.sum(member, axis=1, keepdims=True)

    in_copy.wait()
    in_side = mine[rank:, :] + theirs[half:, :]
    in_tile = jnp.concatenate([in_side] * (128 // rank), axis=0)
    out_copy.wait()
    out_side = mine[keep, :] + theirs[:half, :]
    masked = jnp.concatenate([member * out_side[i : i + 1, :] for i in range(half)], axis=0)
    sums = dot_nt(masked, in_tile)
    per = 128 // rank
    place = lax.broadcasted_iota(jnp.int32, (EX_DEV, 128), 1) // rank
    for g in range(cols // 128):
        block = sums[g * per * EX_DEV : (g * per + 1) * EX_DEV]
        for k in range(1, per):
            row = (g * per + k) * EX_DEV
            block = jnp.where(place == k, sums[row : row + EX_DEV], block)
        e_all[rows, g * 128 : (g + 1) * 128] = block / counts
    e_copies = spread(e_all, e_send, e_recv)
    for copy in e_copies:
        copy.wait()

    everyone = e_all[...]
    part[:, :total] = dot_nt(everyone, everyone)
    k_copy = across(part.at[:, :total], part_in.at[:, :total], p_send.at[0], p_recv.at[0])
    for copy in q_copies:
        copy.wait()
    part[:, total:] = dot_nt(everyone, q_all[...])
    g_copy = across(part.at[:, total:], part_in.at[:, total:], p_send.at[1], p_recv.at[1])
    k_copy.wait()

    gram = (part[:, :total] + part_in[:, :total]) * (1.0 / total)
    r = lax.broadcasted_iota(jnp.int32, (total, total), 0)
    c = lax.broadcasted_iota(jnp.int32, (total, total), 1)
    eye = (r == c).astype(jnp.float32)
    trace = jnp.sum(jnp.sum(gram * eye, axis=1, keepdims=True), axis=0, keepdims=True)
    damping = (0.1 / width) * trace
    gram = gram + damping * eye
    bound = jnp.max(jnp.sum(jnp.abs(gram), axis=0, keepdims=True), axis=1, keepdims=True)
    bound = jnp.minimum(bound, trace + damping) * 1.0001
    low = damping / bound
    y = gram / bound
    for step in range(STEPS):
        scale = 4.0 / ((1.0 + low) * (1.0 + low))
        factor = scale * ((1.0 + low) * eye - y)
        if step == 0:
            y, x = dot(y, factor), factor / bound
        elif step == STEPS - 1:
            x = dot(x, factor)
        else:
            both = dot(jnp.concatenate([y, x], axis=0), factor)
            y, x = both[:total], both[total:]
        low = jnp.minimum(scale * low, 1.0)
    part_in[:, :total] = x
    own = part_in[rows, :total]
    r16 = lax.broadcasted_iota(jnp.int32, (EX_DEV, total), 0)
    c16 = lax.broadcasted_iota(jnp.int32, (EX_DEV, total), 1)
    left = (r16 + me * EX_DEV == c16).astype(jnp.float32) - dot(own, gram)
    own = own + dot(left, x)
    g_copy.wait()
    cross = part[:, total:] + part_in[:, total:]
    out[...] = dot(own, cross) * (1.0 / width ** 0.5)


def dual(n, tokens_in, grad_out, proj_in, proj_out, segment_ids, query_grads):
    tok, rank = tokens_in.shape[0], proj_in.shape[1]
    cols = rank * rank // 2
    total = n * EX_DEV
    dma = pltpu.SemaphoreType.DMA
    return pl.pallas_call(
        functools.partial(kernel, n),
        out_shape=pltpu.VMEM((EX_DEV, total), jnp.float32),
        in_specs=[pl.BlockSpec(memory_space=pl.ANY)] * 6,
        out_specs=pl.BlockSpec(memory_space=pltpu.VMEM),
        scratch_shapes=[
            pltpu.VMEM(tokens_in.shape, jnp.bfloat16),
            pltpu.VMEM(grad_out.shape, jnp.bfloat16),
            pltpu.VMEM(proj_in.shape[::-1], jnp.bfloat16),
            pltpu.VMEM(proj_out.shape[::-1], jnp.bfloat16),
            pltpu.VMEM(segment_ids.shape, jnp.int32),
            pltpu.VMEM((2 * rank, tok), jnp.float32),
            pltpu.VMEM((rank + rank // 2, tok), jnp.float32),
            pltpu.VMEM((total, cols), jnp.float32),
            pltpu.VMEM((total, cols), jnp.float32),
            pltpu.VMEM((total, 2 * total), jnp.float32),
            pltpu.VMEM((total, 2 * total), jnp.float32),
            dma((5,)),
            dma((grad_out.shape[1] // CHUNK,)),
            dma((2,)),
            dma((2,)),
            dma((n - 1,)),
            dma((n - 1,)),
            dma((n - 1,)),
            dma((n - 1,)),
            dma((2,)),
            dma((2,)),
        ],
        compiler_params=pltpu.CompilerParams(
            collective_id=0, has_side_effects=True, vmem_limit_bytes=60 * 2**20
        ),
    )(tokens_in, grad_out, proj_in.T, proj_out.T, segment_ids, query_grads)


def solution(mesh):
    in_specs = (
        P(("grp", "ex"), "ffn"),
        P(("grp", "ex"), "ffn"),
        P("ffn", None),
        P("ffn", None),
        P(("grp", "ex"), None),
        P(("grp", "ex"), None),
    )
    out_specs = P(("grp", "ex"), None)

    def per_device(*args):
        width = args[2].shape[1] ** 2
        n = mesh.shape["ex"]
        if EX_DEV * n == 128 and EX_DEV * n < width and mesh.shape["ffn"] == 2:
            return dual(n, *args)
        return primal(*args)

    return jax.shard_map(
        per_device, mesh=mesh, in_specs=in_specs, out_specs=out_specs, check_vma=False
    )
```
